256 devices in a mesh: region: 64 (over z, x, core), stream: 4 (over y).
Axes of the slice: x: 4, y: 4, z: 8, core: 2. Of those that a mesh axis runs over, the one named last changes fastest.
Arguments:
- crop_features: bfloat16 [512, 256, 2048], P(('region', 'stream')), may hold values from -6 to 6
- crop_counts: int32 [512], P(('region', 'stream')), may hold values from 1 to 256, 43690 in all
- bn_scale: float32 [2048], replicated, may hold values from 0.3 to 3
- bn_shift: float32 [2048], replicated, may hold values from -3 to 3
- projection: bfloat16 [2048, 512], replicated, may hold values from -0.125 to 0.125
- gallery: bfloat16 [512, 3, 32, 512], P(('region', 'stream')), may hold values from -6 to 6
- gallery_fill: int32 [512, 3], P(('region', 'stream')), may hold values from 1 to 32, 64 in all within a row
- adjacency: int32 [512, 128], P(('region', 'stream')), may hold values 0 or 1
Outputs:
- scores: float32 [512, 384, 256], P(('region', 'stream'))
The draws below stay inside these ranges and needn't reach their ends.
Inputs may be any that keep to these rules, and one draw needn't show every extreme that they name: `crop_counts`: each camera has from 1 to 256 live crops; some camera has exactly 256. `gallery_fill`: each track has from 1 to 32 filled frames; every camera has a track with exactly 32.
All inputs are finite; a program needn't handle non-finite values. No bound on the sum of `crop_counts` or of `adjacency` on one device may be relied on, other than what follows from the above.
Results may differ from the reference program's by a relative error of at most 0.0024.
Values may be sent and summed in bfloat16 or wider, within the bound.
A program may use at most 128 MiB of HBM per device.

```python
import math
import jax
import jax.numpy as jnp
import numpy as np
from jax import lax

FEAT = 2048
EMB = 512
TRACKS = 3
FRAMES = 32
CAM_DEV = 2
CAP_CAM = 256
CAMERAS = 512
NEIGH = 128
N_REGION = 64
N_STREAM = 4


def plant(drawn, stream_key, low, largest):
    dims = drawn.shape
    spot = [jax.random.randint(jax.random.fold_in(stream_key, axis), (), 0, dims[axis]) for axis in range(len(dims))]
    drawn = drawn.at[tuple(spot)].set(low)
    longest = dims.index(max(dims))
    spot[longest] = (spot[longest] + 1) % dims[longest]
    return drawn.at[tuple(spot)].set(largest)


def block_scale(key, shape, split, least, high):
    level = 1.0
    for position, parts in split:
        draws = jax.random.uniform(jax.random.fold_in(jax.random.fold_in(key, 6), position), (parts,), jnp.float32, least / len(split), high / len(split))
        level = level * jnp.repeat(jnp.exp(draws), shape[position] // parts).reshape((-1,) + (1,) * (len(shape) - 1 - position))
    return level


def profile(count, total, bound, slope):
    loads = [(1 << 20) // math.isqrt(grade ** slope) + 1 for grade in range(2, count + 1)]
    rest, holding = total - bound - (count - 1), [1] * (count - 1)
    while rest > 0:
        free = [i for i in range(count - 1) if holding[i] < bound]
        whole, remaining = sum([loads[i] for i in free]), rest
        for i in free:
            addition = min(bound - holding[i], max(1, remaining * loads[i] // whole), rest)
            holding[i] = holding[i] + addition
            rest = rest - addition
    return np.array([bound] + holding)


def ragged(key, amount, total, reach, skew):
    if amount == 2:
        one = jax.random.randint(key, (), max(1, total - reach), min(reach, total - 1) + 1)
        return jnp.stack([one, total - one])
    lengths = jnp.asarray(profile(amount, total, reach, skew), jnp.int32)
    couples = (amount - 1) // 2
    giver, receiver = lengths[1:1 + 2 * couples:2], lengths[2:2 + 2 * couples:2]
    margin = jnp.minimum(giver - 1, reach - receiver)
    shifted = jax.random.randint(jax.random.fold_in(key, 1), (couples,), 0, 1 << 20) % (margin + 1)
    lengths = lengths.at[1:1 + 2 * couples:2].set(giver - shifted).at[2:2 + 2 * couples:2].set(receiver + shifted)
    return lengths[jax.random.permutation(jax.random.fold_in(key, 2), amount)]


def centred(stream_key, extent, spread, most, split=(), kind=jnp.bfloat16):
    entries = jax.random.normal(stream_key, extent, jnp.float32) * spread
    if len(split) > 0:
        entries = block_scale(stream_key, extent, split, -0.22, 0.18) * entries
    return jnp.clip(entries, min=-most, max=most).astype(kind)


def setup_inputs(seed: int = 0) -> dict:
    keys = jax.random.split(jax.random.key(seed), 9)
    crop_features = centred(keys[0], (CAMERAS, CAP_CAM, FEAT), 1.0, 6.0, ((0, 256),))
    crop_counts = ragged(keys[1], CAMERAS, CAMERAS * CAP_CAM // 3, CAP_CAM, 2).astype(jnp.int32)
    bn_scale = jnp.clip(jnp.exp(jax.random.uniform(keys[2], (FEAT,), jnp.float32, math.log(0.3), math.log(3.0))), 0.3, 3.0)
    bn_shift = centred(keys[3], (FEAT,), 0.5, 3.0, (), jnp.float32)
    projection = centred(keys[4], (FEAT, EMB), FEAT ** -0.5, 0.125)
    gallery = centred(keys[5], (CAMERAS, TRACKS, FRAMES, EMB), 1.0, 6.0, ((0, 256),))
    gallery_fill = jax.vmap(lambda own: ragged(own, TRACKS, 2 * FRAMES, FRAMES, 1))(jax.random.split(keys[6], CAMERAS)).reshape((CAMERAS, TRACKS)).astype(jnp.int32)
    adjacency = plant((jax.random.randint(keys[7], (CAMERAS, NEIGH), 0, 2) < 1).astype(jnp.int32), jax.random.fold_in(keys[7], 1), 0, 1)
    return dict(crop_features=crop_features, crop_counts=crop_counts, bn_scale=bn_scale, bn_shift=bn_shift, projection=projection, gallery=gallery, gallery_fill=gallery_fill, adjacency=adjacency)


def embed_rows(feature_rows, bn_scale, bn_shift, projection):
    normed = (feature_rows.astype(jnp.float32) * bn_scale + bn_shift).astype(jnp.bfloat16)
    projected = jnp.dot(normed, projection, preferred_element_type=jnp.float32)
    return (projected * lax.rsqrt(lax.optimization_barrier(jnp.sum(projected * projected, axis=-1, keepdims=True)) + 1e-06)).astype(jnp.bfloat16)

def reference(crop_features, crop_counts, bn_scale, bn_shift, projection, gallery, gallery_fill, adjacency):
    dev_total = N_REGION * N_STREAM
    dev_features = crop_features.reshape(dev_total, CAM_DEV * CAP_CAM, FEAT)
    dev_counts = crop_counts.reshape(dev_total, CAM_DEV)
    dev_adjacent = adjacency.reshape(dev_total, CAM_DEV, NEIGH)
    gal_grid = gallery.reshape(N_REGION, N_STREAM, CAM_DEV, TRACKS, FRAMES, EMB)
    fill_grid = gallery_fill.reshape(N_REGION, N_STREAM, CAM_DEV, TRACKS)
    stream_ids = (jnp.arange(dev_total, dtype=jnp.int32) % N_STREAM).astype(jnp.int32)

    def per_device(inputs):
        features_here, counts_here, adjacent_here, stream_here = inputs
        embedding = embed_rows(features_here, bn_scale, bn_shift, projection).reshape(CAM_DEV, CAP_CAM, EMB)
        near_gallery = lax.dynamic_index_in_dim(gal_grid, stream_here, 1, keepdims=False).reshape(NEIGH, TRACKS, FRAMES, EMB)
        near_fill = lax.dynamic_index_in_dim(fill_grid, stream_here, 1, keepdims=False).reshape(NEIGH, TRACKS)
        similarity = jnp.einsum('cpe,nkfe->cnkfp', embedding.astype(jnp.float32), near_gallery.astype(jnp.float32))
        frame_valid = jnp.arange(FRAMES, dtype=jnp.int32)[None, None, :] < near_fill[:, :, None]
        best_score = lax.optimization_barrier(jnp.max(jnp.where(frame_valid[None, :, :, :, None], similarity, -jnp.inf), axis=3))
        live_slots = jnp.arange(CAP_CAM, dtype=jnp.int32)[None, :] < counts_here[:, None]
        weighted = best_score * adjacent_here.astype(jnp.float32)[:, :, None, None]
        weighted = weighted.reshape(CAM_DEV, NEIGH * TRACKS, CAP_CAM)
        return jnp.where(live_slots[:, None, :], weighted, 0.0)
    result = lax.map(per_device, (dev_features, dev_counts, dev_adjacent, stream_ids))
    return result.reshape(CAMERAS, NEIGH * TRACKS, CAP_CAM)
```

```python
import functools

import jax
import jax.numpy as jnp
from jax import lax
from jax.experimental import pallas as pl
from jax.experimental.pallas import tpu as pltpu
from jax.sharding import PartitionSpec as P

MESH = pl.DeviceIdType.MESH
CAMS, CROPS, FEAT, EMB = 2, 256, 2048, 512
TRACKS, FRAMES, KEPT, HALF = 3, 32, 64, 32
NZ, ROWS, NEIGH = 8, 12, 128


def kernel(
    feat, counts, scale, shift, proj, gall, fill, adj, out,
    fv, pv, gv, sc, sh, av, adjc, normed, gal, meta, emb, ro, rss, rsr, rps, rpr,
    lsem, zs, zr, zms, zmr, xs, xr, es, er, ss, sr, ps, pr,
):
    r, s = lax.axis_index("region"), lax.axis_index("stream")
    z, x, c = r // 8, (r // 2) % 4, r % 2
    xi = x % 2
    sib = (r + 1 - 2 * c, s)
    xm = (z * 8 + (x + 1 - 2 * xi) * 2 + c, s)
    pm = (z * 8 + (3 - x) * 2 + c, s)
    pmo = (z * 8 + (3 - x) * 2 + 1 - c, s)
    zp = (((z + 1) % NZ) * 8 + x * 2 + c, s)
    zn = (((z + NZ - 1) % NZ) * 8 + x * 2 + c, s)

    def at(d):
        return (z + d + NZ) % NZ

    local = [
        pltpu.make_async_copy(gall, gv, lsem.at[0]),
        pltpu.make_async_copy(scale, sc, lsem.at[1]),
        pltpu.make_async_copy(shift, sh, lsem.at[2]),
        pltpu.make_async_copy(proj, pv, lsem.at[3]),
        pltpu.make_async_copy(feat.at[0], fv.at[0], lsem.at[4]),
        pltpu.make_async_copy(feat.at[1], fv.at[1], lsem.at[5]),
        pltpu.make_async_copy(adj, av, lsem.at[6]),
    ]
    for cp in local:
        cp.start()
    barrier = pltpu.get_barrier_semaphore()
    peers = (sib, xm, pm, pmo, zp, zn)
    for t in peers:
        pl.semaphore_signal(barrier, inc=1, device_id=t, device_id_type=MESH)

    local[0].wait()
    row = lax.broadcasted_iota(jnp.int32, (KEPT, TRACKS * FRAMES), 0)
    src = lax.broadcasted_iota(jnp.int32, (KEPT, TRACKS * FRAMES), 1)
    notes = []
    for cam in range(CAMS):
        f0, f1 = fill[cam, 0], fill[cam, 1]
        full = jnp.where(f0 == FRAMES, 0, jnp.where(f1 == FRAMES, 1, 2))
        first = jnp.where(full == 0, 1, 0)
        second = jnp.where(full == 2, 1, 2)
        cut = jnp.where(full == 0, f1, f0)
        notes += [cut, full]
        want = jnp.where(
            row < HALF,
            full * FRAMES + row,
            jnp.where(row - HALF < cut, first * FRAMES + row - HALF, second * FRAMES + row - HALF - cut),
        )
        pick = (src == want).astype(jnp.float32).astype(jnp.bfloat16)
        kept = jnp.dot(pick, gv[cam].reshape(TRACKS * FRAMES, EMB), preferred_element_type=jnp.float32)
        gal[z, xi, cam] = kept.astype(jnp.bfloat16)
    line = lax.broadcasted_iota(jnp.int32, (8, 128), 0)
    meta[z, xi] = jnp.where(
        line == 0, notes[0], jnp.where(line == 1, notes[2], jnp.where(line == 2, notes[1], notes[3]))
    )
    pl.semaphore_wait(barrier, len(peers))

    sent = []

    def send(ref_from, ref_to, s_sem, r_sem, to):
        cp = pltpu.make_async_remote_copy(
            src_ref=ref_from, dst_ref=ref_to, send_sem=s_sem, recv_sem=r_sem, device_id=to, device_id_type=MESH
        )
        cp.start()
        sent.append(cp)

    def arrive(ref, s_sem, r_sem):
        pltpu.make_async_remote_copy(
            src_ref=ref, dst_ref=ref, send_sem=s_sem, recv_sem=r_sem, device_id=sib, device_id_type=MESH
        ).wait_recv()

    def unit(stream, zz, part):
        ref = gal.at[zz, 1 - xi if stream == 1 else xi, 1 if stream == 2 else 0]
        return ref if part is None else ref.at[pl.ds(part * HALF, HALF)]

    def note(stream, zz):
        return meta.at[zz, 1 - xi if stream == 1 else xi]

    def z_send(stream, way, hop):
        zz = at(-(hop - 1) if way == 0 else hop - 1)
        ref = unit(stream, zz, way if hop == 4 else None)
        to = zp if way == 0 else zn
        send(ref, ref, zs.at[way, stream, hop - 1], zr.at[way, stream, hop - 1], to)
        if stream < 2 and not (way == 1 and hop == 4):
            ref = note(stream, zz)
            send(ref, ref, zms.at[way, stream, hop - 1], zmr.at[way, stream, hop - 1], to)

    def x_ref(cam, d, part):
        ref = gal.at[at(d), xi, cam]
        return ref if part is None else ref.at[pl.ds(part * HALF, HALF)]

    def x_index(hop, way):
        return 1 if hop == 0 else 2 + (hop - 1) * 2 + way

    def x_send(cam, hop, way):
        k = 0 if cam == 0 else x_index(hop, way)
        ref = x_ref(cam, -hop if way == 0 else hop, way if hop == 4 else None)
        send(ref, ref, xs.at[k], xr.at[k], xm)
        if cam == 0:
            send(meta.at[z, xi], meta.at[z, xi], xs.at[10], xr.at[10], xm)

    def x_arrive(cam, hop, way):
        k = 0 if cam == 0 else x_index(hop, way)
        ref = gal.at[at(-hop if way == 0 else hop), 1 - xi, cam]
        if hop == 4:
            ref = ref.at[pl.ds(way * HALF, HALF)]
        arrive(ref, xs.at[k], xr.at[k])
        if cam == 0:
            arrive(meta.at[z, 1 - xi], xs.at[10], xr.at[10])

    def z_arrive(stream, hop):
        for way in range(2):
            zz = at(-hop if way == 0 else hop)
            arrive(unit(stream, zz, way if hop == 4 else None), zs.at[way, stream, hop - 1], zr.at[way, stream, hop - 1])
            if stream < 2 and not (way == 1 and hop == 4):
                arrive(note(stream, zz), zms.at[way, stream, hop - 1], zmr.at[way, stream, hop - 1])
            if hop < 4:
                z_send(stream, way, hop + 1)
            if stream == 2:
                x_send(1, hop, way)

    z_send(2, 0, 1)
    z_send(2, 1, 1)
    x_send(0, 0, 0)
    z_send(0, 0, 1)
    z_send(0, 1, 1)
    x_send(1, 0, 0)

    def embed(cam):
        rows = fv[cam].astype(jnp.float32) * sc[...].reshape(1, FEAT) + sh[...].reshape(1, FEAT)
        normed[...] = rows.astype(jnp.bfloat16)
        projected = jnp.dot(normed[...], pv[...], preferred_element_type=jnp.float32)
        total = jnp.sum(projected * projected, axis=-1, keepdims=True)
        unit_rows = (projected * lax.rsqrt(total + 1e-06)).astype(jnp.bfloat16)
        emb[0, cam] = unit_rows.T
        send(emb.at[0, cam], emb.at[2, cam], es.at[0, cam], er.at[0, cam], pm)
        send(emb.at[0, cam], emb.at[1, cam], es.at[1, cam], er.at[1, cam], sib)

    local[1].wait()
    local[2].wait()
    local[3].wait()
    local[4].wait()
    embed(0)
    x_arrive(0, 0, 0)
    z_send(1, 0, 1)
    z_send(1, 1, 1)
    local[5].wait()
    embed(1)

    def emb_arrive(grp, cam):
        k = {2: 0, 1: 1, 3: 2}[grp]
        arrive(emb.at[grp, cam], es.at[k, cam], er.at[k, cam])
        if grp == 2:
            send(emb.at[2, cam], emb.at[3, cam], es.at[2, cam], er.at[2, cam], sib)

    def score(zz, grp, cam):
        sims = jnp.dot(
            gal[zz].reshape(4 * KEPT, EMB), emb[grp, cam], preferred_element_type=jnp.float32
        )
        frame = lax.broadcasted_iota(jnp.int32, (HALF, CROPS), 0)
        rows = []
        for q in range(4):
            cut = meta[zz, q // 2, pl.ds(q % 2, 1), :]
            full = meta[zz, q // 2, pl.ds(2 + q % 2, 1), :]
            cut = jnp.concatenate([cut, cut], axis=1)
            full = jnp.concatenate([full, full], axis=1)
            whole = sims[q * KEPT : q * KEPT + HALF]
            mixed = sims[q * KEPT + HALF : (q + 1) * KEPT]
            mine = frame < cut
            a = jnp.max(whole, axis=0, keepdims=True)
            u = jnp.max(jnp.where(mine, mixed, -jnp.inf), axis=0, keepdims=True)
            v = jnp.max(jnp.where(mine, -jnp.inf, mixed), axis=0, keepdims=True)
            rows.append(jnp.where(full == 0, a, u))
            rows.append(jnp.where(full == 1, a, jnp.where(full == 0, u, v)))
            rows.append(jnp.where(full == 2, a, v))
        rows.append(jnp.zeros((4, CROPS), jnp.float32))
        return jnp.concatenate(rows, axis=0)

    def work(hop, grp, cam):
        ways = 1 if hop in (0, 4) else 2

        def body(i, carry):
            zz = at(hop - 2 * hop * i)
            got = score(zz, grp, cam)
            if grp == 0:
                ro[zz, cam] = got
            elif grp == 1:
                rss[zz, cam] = got
            else:
                rps[grp - 2, zz, cam] = got.astype(jnp.bfloat16)
            return carry

        lax.fori_loop(0, ways, body, 0)

    def offsets(hop):
        return ((0, hop),) if hop in (0, 4) else ((0, hop), (1, -hop))

    def give_sib(hop):
        for i, d in offsets(hop):
            k = hop * 2 + i
            send(rss.at[at(d)], rsr.at[at(d)], ss.at[k], sr.at[k], sib)

    def give_pair(hop):
        for t, to in enumerate((pm, pmo)):
            for i, d in offsets(hop):
                k = hop * 2 + i
                send(rps.at[t, at(d)], rpr.at[t, at(d)], ps.at[t, k], pr.at[t, k], to)

    local[6].wait()
    n_row = lax.broadcasted_iota(jnp.int32, (NEIGH * TRACKS, NEIGH), 0)
    n_col = lax.broadcasted_iota(jnp.int32, (NEIGH * TRACKS, NEIGH), 1) * TRACKS
    same = (n_row >= n_col) & (n_row < n_col + TRACKS)
    for cam in range(CAMS):
        spread = jnp.where(same, av[pl.ds(cam, 1), :].astype(jnp.float32), 0.0).astype(jnp.bfloat16)
        adjc[cam] = jnp.dot(spread, jnp.ones((NEIGH, 128), jnp.bfloat16), preferred_element_type=jnp.float32)

    z_arrive(2, 1)
    z_arrive(0, 1)
    x_arrive(1, 0, 0)
    emb_arrive(1, 0)
    emb_arrive(1, 1)
    work(0, 0, 0)
    work(0, 0, 1)
    z_arrive(1, 1)
    work(0, 1, 0)
    work(0, 1, 1)
    give_sib(0)
    x_arrive(1, 1, 0)
    x_arrive(1, 1, 1)
    work(1, 0, 0)
    work(1, 0, 1)
    z_arrive(2, 2)
    work(1, 1, 0)
    work(1, 1, 1)
    give_sib(1)
    z_arrive(0, 2)
    emb_arrive(2, 0)
    z_arrive(1, 2)
    x_arrive(1, 2, 0)
    x_arrive(1, 2, 1)
    work(2, 0, 0)
    work(2, 0, 1)
    z_arrive(2, 3)
    emb_arrive(3, 0)
    work(2, 1, 0)
    work(2, 1, 1)
    give_sib(2)
    work(0, 2, 0)
    work(0, 3, 0)
    z_arrive(0, 3)
    work(1, 2, 0)
    work(1, 3, 0)
    work(2, 2, 0)
    work(2, 3, 0)
    z_arrive(1, 3)
    x_arrive(1, 3, 0)
    x_arrive(1, 3, 1)
    work(3, 0, 0)
    work(3, 0, 1)
    emb_arrive(2, 1)
    z_arrive(2, 4)
    work(3, 1, 0)
    work(3, 1, 1)
    give_sib(3)
    emb_arrive(3, 1)
    for hop in range(3):
        work(hop, 2, 1)
        work(hop, 3, 1)
        give_pair(hop)
    z_arrive(0, 4)
    z_arrive(1, 4)
    for cam in range(CAMS):
        work(3, 2, cam)
        work(3, 3, cam)
    give_pair(3)
    x_arrive(1, 4, 0)
    x_arrive(1, 4, 1)
    for cam in range(CAMS):
        work(4, 2, cam)
        work(4, 3, cam)
    give_pair(4)
    for cam in range(CAMS):
        work(4, 1, cam)
    give_sib(4)
    for cam in range(CAMS):
        work(4, 0, cam)

    lane = lax.broadcasted_iota(jnp.int32, (24, CROPS), 1)

    def weave(even, odd):
        return jnp.concatenate([even[0:6], odd[0:6], even[6:12], odd[6:12]], axis=0)

    def finish(hop):
        for i, d in offsets(hop):
            k = hop * 2 + i
            arrive(rsr.at[at(d)], ss.at[k], sr.at[k])
            for t in range(2):
                arrive(rpr.at[t, at(d)], ps.at[t, k], pr.at[t, k])

        def body(i, carry):
            zz = at(hop - 2 * hop * i)
            for cam in range(CAMS):
                for side in range(2):
                    if side == 0:
                        here, there = ro[zz, cam], rsr[zz, cam]
                    else:
                        here, there = rpr[0, zz, cam].astype(jnp.float32), rpr[1, zz, cam].astype(jnp.float32)
                    block = weave(jnp.where(c == 0, here, there), jnp.where(c == 0, there, here))
                    cls = x // 2 if side == 0 else 1 - x // 2
                    at_row = pl.multiple_of(zz * 48 + cls * 24, 8)
                    factor = adjc[cam, pl.ds(at_row, 24), :]
                    block = block * jnp.concatenate([factor, factor], axis=1)
                    out[cam, pl.ds(at_row, 24), :] = jnp.where(lane < counts[cam], block, 0.0)
            return carry

        lax.fori_loop(0, 1 if hop in (0, 4) else 2, body, 0)

    for hop in range(5):
        finish(hop)
    for cp in sent:
        cp.wait_send()


def per_device(feat, counts, scale, shift, proj, gall, fill, adj):
    hbm = pl.BlockSpec(memory_space=pl.ANY)
    smem = pl.BlockSpec(memory_space=pltpu.SMEM)
    vmem = pl.BlockSpec(memory_space=pltpu.VMEM)
    bf, f32, dma = jnp.bfloat16, jnp.float32, pltpu.SemaphoreType.DMA
    return pl.pallas_call(
        kernel,
        name="match",
        out_shape=jax.ShapeDtypeStruct((CAMS, NEIGH * TRACKS, CROPS), f32),
        in_specs=[hbm, smem, hbm, hbm, hbm, hbm, smem, hbm],
        out_specs=vmem,
        scratch_shapes=[
            pltpu.VMEM((CAMS, CROPS, FEAT), bf),
            pltpu.VMEM((FEAT, EMB), bf),
            pltpu.VMEM((CAMS, TRACKS, FRAMES, EMB), bf),
            pltpu.VMEM((FEAT,), f32),
            pltpu.VMEM((FEAT,), f32),
            pltpu.VMEM((CAMS, NEIGH), jnp.int32),
            pltpu.VMEM((CAMS, NEIGH * TRACKS, 128), f32),
            pltpu.VMEM((CROPS, FEAT), bf),
            pltpu.VMEM((NZ, 2, CAMS, KEPT, EMB), bf),
            pltpu.VMEM((NZ, 2, 8, 128), jnp.int32),
            pltpu.VMEM((4, CAMS, EMB, CROPS), bf),
            pltpu.VMEM((NZ, CAMS, 16, CROPS), f32),
            pltpu.VMEM((NZ, CAMS, 16, CROPS), f32),
            pltpu.VMEM((NZ, CAMS, 16, CROPS), f32),
            pltpu.VMEM((2, NZ, CAMS, 16, CROPS), bf),
            pltpu.VMEM((2, NZ, CAMS, 16, CROPS), bf),
            dma((7,)),
            dma((2, 3, 4)),
            dma((2, 3, 4)),
            dma((2, 2, 4)),
            dma((2, 2, 4)),
            dma((11,)),
            dma((11,)),
            dma((3, CAMS)),
            dma((3, CAMS)),
            dma((10,)),
            dma((10,)),
            dma((2, 10)),
            dma((2, 10)),
        ],
        compiler_params=pltpu.CompilerParams(
            collective_id=0, has_side_effects=True, vmem_limit_bytes=40 * 2**20
        ),
    )(feat, counts, scale, shift, proj, gall, fill, adj)


def solution(mesh):
    return jax.shard_map(
        per_device,
        mesh=mesh,
        in_specs=(
            P(("region", "stream"), None, None),
            P(("region", "stream")),
            P(),
            P(),
            P(),
            P(("region", "stream"), None, None, None),
            P(("region", "stream"), None),
            P(("region", "stream"), None),
        ),
        out_specs=P(("region", "stream"), None, None),
        check_vma=False,
    )
```

```python
import functools

import jax
import jax.numpy as jnp
from jax import lax
from jax.experimental import pallas as pl
from jax.experimental.pallas import tpu as pltpu
from jax.sharding import PartitionSpec as P

MESH = pl.DeviceIdType.MESH
CAMS, CROPS, FEAT, EMB = 2, 256, 2048, 512
TRACKS, FRAMES, KEPT, HALF = 3, 32, 64, 32
NZ, ROWS, NEIGH = 8, 12, 128
DELTA = (0, 1, -1, 2, -2, 3, -3, 4)
SIB_PARTS = ((0, 4), (4, 2), (6, 2))
MESSAGES = (
    ((0, 0), (1, 0), (2, 0), (3, 0)),
    ((0, 1), (1, 1), (2, 1), (3, 1)),
    ((4, 0), (4, 1), (5, 0), (5, 1)),
    ((6, 0), (6, 1), (7, 0), (7, 1)),
)
PLACE = {p: (m, j) for m, part in enumerate(MESSAGES) for j, p in enumerate(part)}


def kernel(
    feat, scale, shift, proj, gall, fill_in, adj, out,
    fill, fv, pv, gv, sc, sh, av, adjc, normed, gal, meta, emb, res, rsr, rps, rpr, outv,
    lsem, zs, zr, ms, mr, xs, xr, es, er, ss, sr, ps, pr, osem,
):
    r, s = lax.axis_index("region"), lax.axis_index("stream")
    z, x, c = r // 8, (r // 2) % 4, r % 2
    xi = x % 2

    def device(z2, x2, c2):
        return (z2 * 8 + x2 * 2 + c2, s)

    sib = device(z, x, 1 - c)
    xm = device(z, x + 1 - 2 * xi, c)
    pm = device(z, 3 - x, c)
    pmo = device(z, 3 - x, 1 - c)
    zp = device((z + 1) % NZ, x, c)
    zn = device((z + NZ - 1) % NZ, x, c)

    def at(d):
        return (z + d + NZ) % NZ

    local = [
        pltpu.make_async_copy(gall, gv, lsem.at[0]),
        pltpu.make_async_copy(fill_in, fill, lsem.at[7]),
        pltpu.make_async_copy(scale, sc, lsem.at[1]),
        pltpu.make_async_copy(shift, sh, lsem.at[2]),
        pltpu.make_async_copy(proj, pv, lsem.at[3]),
        pltpu.make_async_copy(feat.at[0], fv.at[0], lsem.at[4]),
        pltpu.make_async_copy(feat.at[1], fv.at[1], lsem.at[5]),
        pltpu.make_async_copy(adj, av, lsem.at[6]),
    ]
    for cp in local:
        cp.start()
    barrier = pltpu.get_barrier_semaphore()
    peers = (sib, xm, pm, pmo, zp, zn)
    for t in peers:
        pl.semaphore_signal(barrier, inc=1, device_id=t, device_id_type=MESH)

    local[0].wait()
    local[1].wait()
    row = lax.broadcasted_iota(jnp.int32, (KEPT, TRACKS * FRAMES), 0)
    src = lax.broadcasted_iota(jnp.int32, (KEPT, TRACKS * FRAMES), 1)
    notes = []
    for cam in range(CAMS):
        f0, f1 = fill[cam, 0], fill[cam, 1]
        full = jnp.where(f0 == FRAMES, 0, jnp.where(f1 == FRAMES, 1, 2))
        first = jnp.where(full == 0, 1, 0)
        second = jnp.where(full == 2, 1, 2)
        cut = jnp.where(full == 0, f1, f0)
        notes += [cut, full]
        want = jnp.where(
            row < HALF,
            full * FRAMES + row,
            jnp.where(row - HALF < cut, first * FRAMES + row - HALF, second * FRAMES + row - HALF - cut),
        )
        pick = (src == want).astype(jnp.float32).astype(jnp.bfloat16)
        kept = jnp.dot(pick, gv[cam].reshape(TRACKS * FRAMES, EMB), preferred_element_type=jnp.float32)
        gal[z, xi, cam] = kept.astype(jnp.bfloat16)
    line = lax.broadcasted_iota(jnp.int32, (8, 128), 0)
    meta[z, xi] = jnp.where(
        line == 0, notes[0], jnp.where(line == 1, notes[2], jnp.where(line == 2, notes[1], notes[3]))
    )
    pl.semaphore_wait(barrier, len(peers))

    sent = []

    def send(ref_from, ref_to, s_sem, r_sem, to):
        cp = pltpu.make_async_remote_copy(
            src_ref=ref_from, dst_ref=ref_to, send_sem=s_sem, recv_sem=r_sem, device_id=to, device_id_type=MESH
        )
        cp.start()
        sent.append(cp)

    def drain(keep):
        while len(sent) > keep:
            sent.pop(0).wait_send()

    def arrive(ref, s_sem, r_sem):
        pltpu.make_async_remote_copy(
            src_ref=ref, dst_ref=ref, send_sem=s_sem, recv_sem=r_sem, device_id=sib, device_id_type=MESH
        ).wait_recv()

    def unit(stream, zz, part):
        ref = gal.at[zz, 1 - xi if stream == 1 else xi, 1 if stream == 2 else 0]
        return ref if part is None else ref.at[pl.ds(part * HALF, HALF)]

    def note(stream, zz):
        return meta.at[zz, 1 - xi if stream == 1 else xi]

    def noted(stream, way, hop):
        return stream < 2 and not (way == 1 and hop == 4)

    def z_send(stream, way, hop):
        ref = unit(stream, at(-(hop - 1) if way == 0 else hop - 1), way if hop == 4 else None)
        to = zp if way == 0 else zn
        send(ref, ref, zs.at[way, stream, hop - 1], zr.at[way, stream, hop - 1], to)
        if noted(stream, way, hop):
            ref = note(stream, at(-(hop - 1) if way == 0 else hop - 1))
            send(ref, ref, ms.at[way, stream, hop - 1], mr.at[way, stream, hop - 1], to)

    def x_unit(column, cam, hop, way):
        ref = gal.at[at(-hop if way == 0 else hop), column, cam]
        return ref.at[pl.ds(way * HALF, HALF)] if hop == 4 else ref

    def x_index(cam, hop, way):
        return 0 if cam == 0 else 1 if hop == 0 else 2 + (hop - 1) * 2 + way

    def x_send(cam, hop, way):
        k, ref = x_index(cam, hop, way), x_unit(xi, cam, hop, way)
        send(ref, ref, xs.at[k], xr.at[k], xm)
        if cam == 0:
            send(meta.at[z, xi], meta.at[z, xi], xs.at[10], xr.at[10], xm)

    def x_arrive(cam, hop, way):
        k = x_index(cam, hop, way)
        arrive(x_unit(1 - xi, cam, hop, way), xs.at[k], xr.at[k])
        if cam == 0:
            arrive(meta.at[z, 1 - xi], xs.at[10], xr.at[10])

    def z_arrive(stream, hop):
        for way in range(2):
            zz = at(-hop if way == 0 else hop)
            arrive(unit(stream, zz, way if hop == 4 else None), zs.at[way, stream, hop - 1], zr.at[way, stream, hop - 1])
            if noted(stream, way, hop):
                arrive(note(stream, zz), ms.at[way, stream, hop - 1], mr.at[way, stream, hop - 1])
            if hop < 4:
                z_send(stream, way, hop + 1)
            if stream == 2:
                x_send(1, hop, way)

    def embed(cam):
        rows = fv[cam].astype(jnp.float32) * sc[...].reshape(1, FEAT) + sh[...].reshape(1, FEAT)
        normed[...] = rows.astype(jnp.bfloat16)
        projected = jnp.dot(normed[...], pv[...], preferred_element_type=jnp.float32)
        total = jnp.sum(projected * projected, axis=-1, keepdims=True)
        unit_rows = (projected * lax.rsqrt(total + 1e-06)).astype(jnp.bfloat16)
        emb[0, cam] = unit_rows.T

    def emb_send(grp, cam):
        k, to = {2: (0, pm), 1: (1, sib)}[grp]
        send(emb.at[0, cam], emb.at[grp, cam], es.at[k, cam], er.at[k, cam], to)

    def emb_arrive(grp, cam):
        k = {2: 0, 1: 1, 3: 2}[grp]
        arrive(emb.at[grp, cam], es.at[k, cam], er.at[k, cam])
        if grp == 2:
            send(emb.at[2, cam], emb.at[3, cam], es.at[2, cam], er.at[2, cam], sib)

    def score(zz, grp, cam):
        sims = jnp.dot(
            gal[zz].reshape(4 * KEPT, EMB), emb[grp, cam], preferred_element_type=jnp.float32
        )
        frame = lax.broadcasted_iota(jnp.int32, (HALF, CROPS), 0)
        rows = []
        for q in range(4):
            cut = meta[zz, q // 2, pl.ds(q % 2, 1), :]
            full = meta[zz, q // 2, pl.ds(2 + q % 2, 1), :]
            cut = jnp.concatenate([cut, cut], axis=1)
            full = jnp.concatenate([full, full], axis=1)
            whole = sims[q * KEPT : q * KEPT + HALF]
            mixed = sims[q * KEPT + HALF : (q + 1) * KEPT]
            mine = frame < cut
            a = jnp.max(whole, axis=0, keepdims=True)
            u = jnp.max(jnp.where(mine, mixed, -jnp.inf), axis=0, keepdims=True)
            v = jnp.max(jnp.where(mine, -jnp.inf, mixed), axis=0, keepdims=True)
            rows.append(jnp.where(full == 0, a, u))
            rows.append(jnp.where(full == 1, a, jnp.where(full == 0, u, v)))
            rows.append(jnp.where(full == 2, a, v))
        rows.append(jnp.zeros((4, CROPS), jnp.float32))
        return jnp.concatenate(rows, axis=0)

    def work(places, grps, cams):
        ng, nc = grps[1] - grps[0], cams[1] - cams[0]

        def body(t, carry):
            i = places[0] + t // (ng * nc)
            grp, cam = grps[0] + (t // nc) % ng, cams[0] + t % nc
            d = jnp.where(i % 2 == 1, (i + 1) // 2, 0 - i // 2)
            res[grp, i, cam] = score(at(d), grp, cam)
            return carry

        count = (places[1] - places[0]) * ng * nc
        lax.fori_loop(0, count, body, 0, unroll=min(count, 4))

    def give_sib(k):
        lo, n = SIB_PARTS[k]
        send(res.at[1, pl.ds(lo, n)], rsr.at[pl.ds(lo, n)], ss.at[k], sr.at[k], sib)

    def give_pair(m):
        for t, to in enumerate((pm, pmo)):
            rows = [res[2 + t, i, cam][0:ROWS] for i, cam in MESSAGES[m]]
            rps[t, m] = jnp.concatenate(rows, axis=0).astype(jnp.bfloat16)
            send(rps.at[t, m], rpr.at[t, m], ps.at[t, m], pr.at[t, m], to)

    x_send(0, 0, 0)
    z_send(2, 0, 1)
    z_send(2, 1, 1)
    local[2].wait()
    local[3].wait()
    local[4].wait()
    local[5].wait()
    embed(0)
    emb_send(2, 0)
    z_send(0, 0, 1)
    z_send(0, 1, 1)
    x_send(1, 0, 0)
    emb_send(1, 0)
    local[6].wait()
    embed(1)
    emb_send(1, 1)
    x_arrive(0, 0, 0)
    z_send(1, 0, 1)
    z_send(1, 1, 1)

    local[7].wait()
    n_row = lax.broadcasted_iota(jnp.int32, (NEIGH * TRACKS, NEIGH), 0)
    n_col = lax.broadcasted_iota(jnp.int32, (NEIGH * TRACKS, NEIGH), 1) * TRACKS
    same = (n_row >= n_col) & (n_row < n_col + TRACKS)
    for cam in range(CAMS):
        spread = jnp.where(same, av[pl.ds(cam, 1), :].astype(jnp.float32), 0.0).astype(jnp.bfloat16)
        adjc[cam] = jnp.dot(spread, jnp.ones((NEIGH, 128), jnp.bfloat16), preferred_element_type=jnp.float32)

    own, other, all_cams, pair = (0, 1), (1, 2), (0, 2), (2, 4)
    z_arrive(2, 1)
    emb_send(2, 1)
    z_arrive(0, 1)
    x_arrive(1, 0, 0)
    emb_arrive(1, 0)
    emb_arrive(1, 1)
    work((0, 1), (0, 2), all_cams)
    z_arrive(1, 1)
    z_arrive(2, 2)
    x_arrive(1, 1, 0)
    x_arrive(1, 1, 1)
    work((1, 3), own, all_cams)
    z_arrive(0, 2)
    work((1, 3), other, all_cams)
    emb_arrive(2, 0)
    z_arrive(1, 2)
    z_arrive(2, 3)
    emb_arrive(3, 0)
    work((0, 3), pair, (0, 1))
    x_arrive(1, 2, 0)
    x_arrive(1, 2, 1)
    work((3, 4), pair, (0, 1))
    give_pair(0)
    z_arrive(0, 3)
    work((3, 5), own, all_cams)
    work((4, 5), pair, (0, 1))
    emb_arrive(2, 1)
    z_arrive(1, 3)
    work((3, 5), other, all_cams)
    give_sib(0)
    z_arrive(2, 4)
    emb_arrive(3, 1)
    work((0, 4), pair, (1, 2))
    give_pair(1)
    x_arrive(1, 3, 0)
    x_arrive(1, 3, 1)
    work((4, 5), pair, (1, 2))
    work((5, 6), pair, all_cams)
    give_pair(2)
    z_arrive(0, 4)
    work((6, 7), pair, all_cams)
    work((5, 7), (0, 2), all_cams)
    give_sib(1)
    drain(20)
    z_arrive(1, 4)
    x_arrive(1, 4, 0)
    x_arrive(1, 4, 1)
    work((7, 8), pair, all_cams)
    give_pair(3)
    work((7, 8), other, all_cams)
    give_sib(2)
    work((7, 8), own, all_cams)
    drain(6)

    def weave(even, odd):
        return jnp.concatenate([even[0:6], odd[0:6], even[6:12], odd[6:12]], axis=0)

    written = []

    def finish(i):
        zz = at(DELTA[i])
        for cam in range(CAMS):
            m, j = PLACE[i, cam]
            for side in range(2):
                if side == 0:
                    here, there = res[0, i, cam], rsr[i, cam]
                else:
                    here, there = [rpr[t, m, j * ROWS : (j + 1) * ROWS].astype(jnp.float32) for t in range(2)]
                block = weave(jnp.where(c == 0, here, there), jnp.where(c == 0, there, here))
                cls = x // 2 if side == 0 else 1 - x // 2
                at_row = pl.multiple_of(zz * 48 + cls * 24, 8)
                factor = adjc[cam, pl.ds(at_row, 24), :]
                outv[cam, pl.ds(at_row, 24), :] = block * jnp.concatenate([factor, factor], axis=1)
        rows = pl.ds(pl.multiple_of(zz * 48, 8), 48)
        for cam in range(CAMS):
            cp = pltpu.make_async_copy(outv.at[cam, rows], out.at[cam, rows], osem.at[i, cam])
            cp.start()
            written.append(cp)

    def pair_arrive(m):
        for t in range(2):
            arrive(rpr.at[t, m], ps.at[t, m], pr.at[t, m])

    def sib_arrive(k):
        lo, n = SIB_PARTS[k]
        arrive(rsr.at[pl.ds(lo, n)], ss.at[k], sr.at[k])

    sib_arrive(0)
    pair_arrive(0)
    pair_arrive(1)
    for i in range(4):
        finish(i)
    sib_arrive(1)
    pair_arrive(2)
    for i in (4, 5):
        finish(i)
    sib_arrive(2)
    pair_arrive(3)
    for i in (6, 7):
        finish(i)
    drain(0)
    for cp in written:
        cp.wait()


def per_device(feat, counts, scale, shift, proj, gall, fill, adj):
    hbm = pl.BlockSpec(memory_space=pltpu.HBM)
    bf, f32, dma = jnp.bfloat16, jnp.float32, pltpu.SemaphoreType.DMA
    scores = pl.pallas_call(
        kernel,
        name="match",
        out_shape=jax.ShapeDtypeStruct((CAMS, NEIGH * TRACKS, CROPS), f32),
        in_specs=[hbm] * 7,
        out_specs=hbm,
        scratch_shapes=[
            pltpu.SMEM((CAMS, TRACKS), jnp.int32),
            pltpu.VMEM((CAMS, CROPS, FEAT), bf),
            pltpu.VMEM((FEAT, EMB), bf),
            pltpu.VMEM((CAMS, TRACKS, FRAMES, EMB), bf),
            pltpu.VMEM((FEAT,), f32),
            pltpu.VMEM((FEAT,), f32),
            pltpu.VMEM((CAMS, NEIGH), jnp.int32),
            pltpu.VMEM((CAMS, NEIGH * TRACKS, 128), f32),
            pltpu.VMEM((CROPS, FEAT), bf),
            pltpu.VMEM((NZ, 2, CAMS, KEPT, EMB), bf),
            pltpu.VMEM((NZ, 2, 8, 128), jnp.int32),
            pltpu.VMEM((4, CAMS, EMB, CROPS), bf),
            pltpu.VMEM((4, NZ, CAMS, 16, CROPS), f32),
            pltpu.VMEM((NZ, CAMS, 16, CROPS), f32),
            pltpu.VMEM((2, 4, 4 * ROWS, CROPS), bf),
            pltpu.VMEM((2, 4, 4 * ROWS, CROPS), bf),
            pltpu.VMEM((CAMS, NEIGH * TRACKS, CROPS), f32),
            dma((8,)),
            dma((2, 3, 4)),
            dma((2, 3, 4)),
            dma((2, 2, 4)),
            dma((2, 2, 4)),
            dma((11,)),
            dma((11,)),
            dma((3, CAMS)),
            dma((3, CAMS)),
            dma((3,)),
            dma((3,)),
            dma((2, 4)),
            dma((2, 4)),
            dma((NZ, CAMS)),
        ],
        compiler_params=pltpu.CompilerParams(
            collective_id=0, has_side_effects=True, vmem_limit_bytes=60 * 2**20
        ),
    )(feat, scale, shift, proj, gall, fill, adj)
    live = jnp.arange(CROPS, dtype=jnp.int32)[None, :] < counts[:, None]
    return jnp.where(live[:, None, :], scores, 0.0)


def solution(mesh):
    return jax.shard_map(
        per_device,
        mesh=mesh,
        in_specs=(
            P(("region", "stream"), None, None),
            P(("region", "stream")),
            P(),
            P(),
            P(),
            P(("region", "stream"), None, None, None),
            P(("region", "stream"), None),
            P(("region", "stream"), None),
        ),
        out_specs=P(("region", "stream"), None, None),
        check_vma=False,
    )
```

```python
import functools

import jax
import jax.numpy as jnp
from jax import lax
from jax.experimental import pallas as pl
from jax.experimental.pallas import tpu as pltpu
from jax.sharding import PartitionSpec as P

MESH = pl.DeviceIdType.MESH
CAMS, CROPS, FEAT, EMB = 2, 256, 2048, 512
TRACKS, FRAMES, KEPT, HALF = 3, 32, 64, 32
NZ, ROWS, NEIGH = 8, 12, 128
DELTA = (0, 1, -1, 2, -2, 3, -3, 4)
SIB_PARTS = ((0, 4), (4, 2), (6, 2))
MESSAGES = (
    ((0, 0), (1, 0), (2, 0), (3, 0)),
    ((0, 1), (1, 1), (2, 1), (3, 1)),
    ((4, 0), (4, 1), (5, 0), (5, 1)),
    ((6, 0), (6, 1), (7, 0), (7, 1)),
)
PLACE = {p: (m, j) for m, part in enumerate(MESSAGES) for j, p in enumerate(part)}


def kernel(
    feat, counts_in, scale, shift, proj, gall, fill_in, adj, out,
    counts, fill, fv, pv, gv, sc, sh, av, adjc, normed, gal, meta, emb, res, rsr, rps, rpr,
    lsem, zs, zr, ms, mr, xs, xr, es, er, ss, sr, ps, pr,
):
    r, s = lax.axis_index("region"), lax.axis_index("stream")
    z, x, c = r // 8, (r // 2) % 4, r % 2
    xi = x % 2

    def device(z2, x2, c2):
        return (z2 * 8 + x2 * 2 + c2, s)

    sib = device(z, x, 1 - c)
    xm = device(z, x + 1 - 2 * xi, c)
    pm = device(z, 3 - x, c)
    pmo = device(z, 3 - x, 1 - c)
    zp = device((z + 1) % NZ, x, c)
    zn = device((z + NZ - 1) % NZ, x, c)

    def at(d):
        return (z + d + NZ) % NZ

    local = [
        pltpu.make_async_copy(gall, gv, lsem.at[0]),
        pltpu.make_async_copy(fill_in, fill, lsem.at[7]),
        pltpu.make_async_copy(scale, sc, lsem.at[1]),
        pltpu.make_async_copy(shift, sh, lsem.at[2]),
        pltpu.make_async_copy(proj, pv, lsem.at[3]),
        pltpu.make_async_copy(feat.at[0], fv.at[0], lsem.at[4]),
        pltpu.make_async_copy(feat.at[1], fv.at[1], lsem.at[5]),
        pltpu.make_async_copy(adj, av, lsem.at[6]),
        pltpu.make_async_copy(counts_in, counts, lsem.at[8]),
    ]
    for cp in local:
        cp.start()
    barrier = pltpu.get_barrier_semaphore()
    peers = (sib, xm, pm, pmo, zp, zn)
    for t in peers:
        pl.semaphore_signal(barrier, inc=1, device_id=t, device_id_type=MESH)

    local[0].wait()
    local[1].wait()
    row = lax.broadcasted_iota(jnp.int32, (KEPT, TRACKS * FRAMES), 0)
    src = lax.broadcasted_iota(jnp.int32, (KEPT, TRACKS * FRAMES), 1)
    notes = []
    for cam in range(CAMS):
        f0, f1 = fill[cam, 0], fill[cam, 1]
        full = jnp.where(f0 == FRAMES, 0, jnp.where(f1 == FRAMES, 1, 2))
        first = jnp.where(full == 0, 1, 0)
        second = jnp.where(full == 2, 1, 2)
        cut = jnp.where(full == 0, f1, f0)
        notes += [cut, full]
        want = jnp.where(
            row < HALF,
            full * FRAMES + row,
            jnp.where(row - HALF < cut, first * FRAMES + row - HALF, second * FRAMES + row - HALF - cut),
        )
        pick = (src == want).astype(jnp.float32).astype(jnp.bfloat16)
        kept = jnp.dot(pick, gv[cam].reshape(TRACKS * FRAMES, EMB), preferred_element_type=jnp.float32)
        gal[z, xi, cam] = kept.astype(jnp.bfloat16)
    line = lax.broadcasted_iota(jnp.int32, (8, 128), 0)
    meta[z, xi] = jnp.where(
        line == 0, notes[0], jnp.where(line == 1, notes[2], jnp.where(line == 2, notes[1], notes[3]))
    )
    pl.semaphore_wait(barrier, len(peers))

    sent = []

    def send(ref_from, ref_to, s_sem, r_sem, to):
        cp = pltpu.make_async_remote_copy(
            src_ref=ref_from, dst_ref=ref_to, send_sem=s_sem, recv_sem=r_sem, device_id=to, device_id_type=MESH
        )
        cp.start()
        sent.append(cp)

    def drain(keep):
        while len(sent) > keep:
            sent.pop(0).wait_send()

    def arrive(ref, s_sem, r_sem):
        pltpu.make_async_remote_copy(
            src_ref=ref, dst_ref=ref, send_sem=s_sem, recv_sem=r_sem, device_id=sib, device_id_type=MESH
        ).wait_recv()

    def unit(stream, zz, part):
        ref = gal.at[zz, 1 - xi if stream == 1 else xi, 1 if stream == 2 else 0]
        return ref if part is None else ref.at[pl.ds(part * HALF, HALF)]

    def note(stream, zz):
        return meta.at[zz, 1 - xi if stream == 1 else xi]

    def noted(stream, way, hop):
        return stream < 2 and not (way == 1 and hop == 4)

    def z_send(stream, way, hop):
        ref = unit(stream, at(-(hop - 1) if way == 0 else hop - 1), way if hop == 4 else None)
        to = zp if way == 0 else zn
        send(ref, ref, zs.at[way, stream, hop - 1], zr.at[way, stream, hop - 1], to)
        if noted(stream, way, hop):
            ref = note(stream, at(-(hop - 1) if way == 0 else hop - 1))
            send(ref, ref, ms.at[way, stream, hop - 1], mr.at[way, stream, hop - 1], to)

    def x_unit(column, cam, hop, way):
        ref = gal.at[at(-hop if way == 0 else hop), column, cam]
        return ref.at[pl.ds(way * HALF, HALF)] if hop == 4 else ref

    def x_index(cam, hop, way):
        return 0 if cam == 0 else 1 if hop == 0 else 2 + (hop - 1) * 2 + way

    def x_send(cam, hop, way):
        k, ref = x_index(cam, hop, way), x_unit(xi, cam, hop, way)
        send(ref, ref, xs.at[k], xr.at[k], xm)
        if cam == 0:
            send(meta.at[z, xi], meta.at[z, xi], xs.at[10], xr.at[10], xm)

    def x_arrive(cam, hop, way):
        k = x_index(cam, hop, way)
        arrive(x_unit(1 - xi, cam, hop, way), xs.at[k], xr.at[k])
        if cam == 0:
            arrive(meta.at[z, 1 - xi], xs.at[10], xr.at[10])

    def z_arrive(stream, hop):
        for way in range(2):
            zz = at(-hop if way == 0 else hop)
            arrive(unit(stream, zz, way if hop == 4 else None), zs.at[way, stream, hop - 1], zr.at[way, stream, hop - 1])
            if noted(stream, way, hop):
                arrive(note(stream, zz), ms.at[way, stream, hop - 1], mr.at[way, stream, hop - 1])
            if hop < 4:
                z_send(stream, way, hop + 1)
            if stream == 2:
                x_send(1, hop, way)

    def embed(cam):
        rows = fv[cam].astype(jnp.float32) * sc[...].reshape(1, FEAT) + sh[...].reshape(1, FEAT)
        normed[...] = rows.astype(jnp.bfloat16)
        projected = jnp.dot(normed[...], pv[...], preferred_element_type=jnp.float32)
        total = jnp.sum(projected * projected, axis=-1, keepdims=True)
        unit_rows = (projected * lax.rsqrt(total + 1e-06)).astype(jnp.bfloat16)
        emb[0, cam] = unit_rows.T

    def emb_send(grp, cam):
        k, to = {2: (0, pm), 1: (1, sib)}[grp]
        send(emb.at[0, cam], emb.at[grp, cam], es.at[k, cam], er.at[k, cam], to)

    def emb_arrive(grp, cam):
        k = {2: 0, 1: 1, 3: 2}[grp]
        arrive(emb.at[grp, cam], es.at[k, cam], er.at[k, cam])
        if grp == 2:
            send(emb.at[2, cam], emb.at[3, cam], es.at[2, cam], er.at[2, cam], sib)

    def score(zz, grp, cam):
        sims = jnp.dot(
            gal[zz].reshape(4 * KEPT, EMB), emb[grp, cam], preferred_element_type=jnp.float32
        )
        frame = lax.broadcasted_iota(jnp.int32, (HALF, CROPS), 0)
        rows = []
        for q in range(4):
            cut = meta[zz, q // 2, pl.ds(q % 2, 1), :]
            full = meta[zz, q // 2, pl.ds(2 + q % 2, 1), :]
            cut = jnp.concatenate([cut, cut], axis=1)
            full = jnp.concatenate([full, full], axis=1)
            whole = sims[q * KEPT : q * KEPT + HALF]
            mixed = sims[q * KEPT + HALF : (q + 1) * KEPT]
            mine = frame < cut
            a = jnp.max(whole, axis=0, keepdims=True)
            u = jnp.max(jnp.where(mine, mixed, -jnp.inf), axis=0, keepdims=True)
            v = jnp.max(jnp.where(mine, -jnp.inf, mixed), axis=0, keepdims=True)
            rows.append(jnp.where(full == 0, a, u))
            rows.append(jnp.where(full == 1, a, jnp.where(full == 0, u, v)))
            rows.append(jnp.where(full == 2, a, v))
        rows.append(jnp.zeros((4, CROPS), jnp.float32))
        return jnp.concatenate(rows, axis=0)

    def work(places, grps, cams):
        ng, nc = grps[1] - grps[0], cams[1] - cams[0]

        def body(t, carry):
            i = places[0] + t // (ng * nc)
            grp, cam = grps[0] + (t // nc) % ng, cams[0] + t % nc
            d = jnp.where(i % 2 == 1, (i + 1) // 2, 0 - i // 2)
            res[grp, i, cam] = score(at(d), grp, cam)
            return carry

        count = (places[1] - places[0]) * ng * nc
        lax.fori_loop(0, count, body, 0, unroll=min(count, 4))

    def give_sib(k):
        lo, n = SIB_PARTS[k]
        send(res.at[1, pl.ds(lo, n)], rsr.at[pl.ds(lo, n)], ss.at[k], sr.at[k], sib)

    def give_pair(m):
        for t, to in enumerate((pm, pmo)):
            rows = [res[2 + t, i, cam][0:ROWS] for i, cam in MESSAGES[m]]
            rps[t, m] = jnp.concatenate(rows, axis=0).astype(jnp.bfloat16)
            send(rps.at[t, m], rpr.at[t, m], ps.at[t, m], pr.at[t, m], to)

    x_send(0, 0, 0)
    z_send(2, 0, 1)
    z_send(2, 1, 1)
    local[2].wait()
    local[3].wait()
    local[4].wait()
    local[5].wait()
    embed(0)
    emb_send(2, 0)
    z_send(0, 0, 1)
    z_send(0, 1, 1)
    x_send(1, 0, 0)
    emb_send(1, 0)
    local[6].wait()
    embed(1)
    emb_send(1, 1)
    x_arrive(0, 0, 0)
    z_send(1, 0, 1)
    z_send(1, 1, 1)

    local[7].wait()
    local[8].wait()
    n_row = lax.broadcasted_iota(jnp.int32, (NEIGH * TRACKS, NEIGH), 0)
    n_col = lax.broadcasted_iota(jnp.int32, (NEIGH * TRACKS, NEIGH), 1) * TRACKS
    same = (n_row >= n_col) & (n_row < n_col + TRACKS)
    for cam in range(CAMS):
        spread = jnp.where(same, av[pl.ds(cam, 1), :].astype(jnp.float32), 0.0).astype(jnp.bfloat16)
        adjc[cam] = jnp.dot(spread, jnp.ones((NEIGH, 128), jnp.bfloat16), preferred_element_type=jnp.float32)

    own, other, all_cams, pair = (0, 1), (1, 2), (0, 2), (2, 4)
    z_arrive(2, 1)
    emb_send(2, 1)
    z_arrive(0, 1)
    x_arrive(1, 0, 0)
    emb_arrive(1, 0)
    emb_arrive(1, 1)
    work((0, 1), (0, 2), all_cams)
    z_arrive(1, 1)
    z_arrive(2, 2)
    x_arrive(1, 1, 0)
    x_arrive(1, 1, 1)
    work((1, 3), own, all_cams)
    z_arrive(0, 2)
    work((1, 3), other, all_cams)
    emb_arrive(2, 0)
    z_arrive(1, 2)
    z_arrive(2, 3)
    emb_arrive(3, 0)
    work((0, 3), pair, (0, 1))
    x_arrive(1, 2, 0)
    x_arrive(1, 2, 1)
    work((3, 4), pair, (0, 1))
    give_pair(0)
    z_arrive(0, 3)
    work((3, 5), own, all_cams)
    work((4, 5), pair, (0, 1))
    emb_arrive(2, 1)
    z_arrive(1, 3)
    work((3, 5), other, all_cams)
    give_sib(0)
    z_arrive(2, 4)
    emb_arrive(3, 1)
    work((0, 4), pair, (1, 2))
    give_pair(1)
    x_arrive(1, 3, 0)
    x_arrive(1, 3, 1)
    work((4, 5), pair, (1, 2))
    work((5, 6), pair, all_cams)
    give_pair(2)
    z_arrive(0, 4)
    work((6, 7), pair, all_cams)
    work((5, 7), (0, 2), all_cams)
    give_sib(1)
    drain(20)
    z_arrive(1, 4)
    x_arrive(1, 4, 0)
    x_arrive(1, 4, 1)
    work((7, 8), pair, all_cams)
    give_pair(3)
    work((7, 8), other, all_cams)
    give_sib(2)
    work((7, 8), own, all_cams)
    drain(6)

    def weave(even, odd):
        return jnp.concatenate([even[0:6], odd[0:6], even[6:12], odd[6:12]], axis=0)

    lane = lax.broadcasted_iota(jnp.int32, (24, CROPS), 1)

    def finish(i):
        zz = at(DELTA[i])
        for cam in range(CAMS):
            m, j = PLACE[i, cam]
            for side in range(2):
                if side == 0:
                    here, there = res[0, i, cam], rsr[i, cam]
                else:
                    here, there = [rpr[t, m, j * ROWS : (j + 1) * ROWS].astype(jnp.float32) for t in range(2)]
                block = weave(jnp.where(c == 0, here, there), jnp.where(c == 0, there, here))
                cls = x // 2 if side == 0 else 1 - x // 2
                at_row = pl.multiple_of(zz * 48 + cls * 24, 8)
                factor = adjc[cam, pl.ds(at_row, 24), :]
                block = block * jnp.concatenate([factor, factor], axis=1)
                out[cam, pl.ds(at_row, 24), :] = jnp.where(lane < counts[cam], block, 0.0)

    def pair_arrive(m):
        for t in range(2):
            arrive(rpr.at[t, m], ps.at[t, m], pr.at[t, m])

    def sib_arrive(k):
        lo, n = SIB_PARTS[k]
        arrive(rsr.at[pl.ds(lo, n)], ss.at[k], sr.at[k])

    sib_arrive(0)
    pair_arrive(0)
    pair_arrive(1)
    for i in range(4):
        finish(i)
    sib_arrive(1)
    pair_arrive(2)
    for i in (4, 5):
        finish(i)
    sib_arrive(2)
    pair_arrive(3)
    for i in (6, 7):
        finish(i)
    drain(0)


def per_device(feat, counts, scale, shift, proj, gall, fill, adj):
    hbm = pl.BlockSpec(memory_space=pltpu.HBM)
    bf, f32, dma = jnp.bfloat16, jnp.float32, pltpu.SemaphoreType.DMA
    return pl.pallas_call(
        kernel,
        name="match",
        out_shape=pltpu.VMEM((CAMS, NEIGH * TRACKS, CROPS), f32),
        in_specs=[hbm] * 8,
        out_specs=pl.BlockSpec(memory_space=pltpu.VMEM),
        scratch_shapes=[
            pltpu.SMEM((CAMS,), jnp.int32),
            pltpu.SMEM((CAMS, TRACKS), jnp.int32),
            pltpu.VMEM((CAMS, CROPS, FEAT), bf),
            pltpu.VMEM((FEAT, EMB), bf),
            pltpu.VMEM((CAMS, TRACKS, FRAMES, EMB), bf),
            pltpu.VMEM((FEAT,), f32),
            pltpu.VMEM((FEAT,), f32),
            pltpu.VMEM((CAMS, NEIGH), jnp.int32),
            pltpu.VMEM((CAMS, NEIGH * TRACKS, 128), f32),
            pltpu.VMEM((CROPS, FEAT), bf),
            pltpu.VMEM((NZ, 2, CAMS, KEPT, EMB), bf),
            pltpu.VMEM((NZ, 2, 8, 128), jnp.int32),
            pltpu.VMEM((4, CAMS, EMB, CROPS), bf),
            pltpu.VMEM((4, NZ, CAMS, 16, CROPS), f32),
            pltpu.VMEM((NZ, CAMS, 16, CROPS), f32),
            pltpu.VMEM((2, 4, 4 * ROWS, CROPS), bf),
            pltpu.VMEM((2, 4, 4 * ROWS, CROPS), bf),
            dma((9,)),
            dma((2, 3, 4)),
            dma((2, 3, 4)),
            dma((2, 2, 4)),
            dma((2, 2, 4)),
            dma((11,)),
            dma((11,)),
            dma((3, CAMS)),
            dma((3, CAMS)),
            dma((3,)),
            dma((3,)),
            dma((2, 4)),
            dma((2, 4)),
        ],
        compiler_params=pltpu.CompilerParams(
            collective_id=0, has_side_effects=True, vmem_limit_bytes=60 * 2**20
        ),
    )(feat, counts, scale, shift, proj, gall, fill, adj)


def solution(mesh):
    return jax.shard_map(
        per_device,
        mesh=mesh,
        in_specs=(
            P(("region", "stream"), None, None),
            P(("region", "stream")),
            P(),
            P(),
            P(),
            P(("region", "stream"), None, None, None),
            P(("region", "stream"), None),
            P(("region", "stream"), None),
        ),
        out_specs=P(("region", "stream"), None, None),
        check_vma=False,
    )
```

```python
import functools

import jax
import jax.numpy as jnp
from jax import lax
from jax.experimental import pallas as pl
from jax.experimental.pallas import tpu as pltpu
from jax.sharding import PartitionSpec as P

MESH = pl.DeviceIdType.MESH
CAMS, CROPS, FEAT, EMB = 2, 256, 2048, 512
TRACKS, FRAMES, KEPT, HALF = 3, 32, 64, 32
NZ, ROWS, NEIGH = 8, 12, 128
DELTA = (0, 1, -1, 2, -2, 3, -3, 4)
SIB_PARTS = ((0, 4), (4, 2), (6, 2))
MESSAGES = (
    ((0, 0), (1, 0), (2, 0), (3, 0)),
    ((0, 1), (1, 1), (2, 1), (3, 1)),
    ((4, 0), (4, 1), (5, 0), (5, 1)),
    ((6, 0), (6, 1), (7, 0), (7, 1)),
)
PLACE = {p: (m, j) for m, part in enumerate(MESSAGES) for j, p in enumerate(part)}


def kernel(
    feat, counts_in, scale, shift, proj, gall, fill_in, adj, out,
    counts, fill, fv, pv, gv, sc, sh, av, adjc, normed, gal, meta, emb, res, rsr, rps, rpr,
    lsem, zs, zr, ms, mr, xs, xr, es, er, ss, sr, ps, pr,
):
    r, s = lax.axis_index("region"), lax.axis_index("stream")
    z, x, c = r // 8, (r // 2) % 4, r % 2
    xi = x % 2

    def device(z2, x2, c2):
        return (z2 * 8 + x2 * 2 + c2, s)

    sib = device(z, x, 1 - c)
    xm = device(z, x + 1 - 2 * xi, c)
    pm = device(z, 3 - x, c)
    pmo = device(z, 3 - x, 1 - c)
    zp = device((z + 1) % NZ, x, c)
    zn = device((z + NZ - 1) % NZ, x, c)

    def at(d):
        return (z + d + NZ) % NZ

    local = [
        pltpu.make_async_copy(gall, gv, lsem.at[0]),
        pltpu.make_async_copy(fill_in, fill, lsem.at[7]),
        pltpu.make_async_copy(scale, sc, lsem.at[1]),
        pltpu.make_async_copy(shift, sh, lsem.at[2]),
        pltpu.make_async_copy(proj, pv, lsem.at[3]),
        pltpu.make_async_copy(feat.at[0], fv.at[0], lsem.at[4]),
        pltpu.make_async_copy(feat.at[1], fv.at[1], lsem.at[5]),
        pltpu.make_async_copy(adj, av, lsem.at[6]),
        pltpu.make_async_copy(counts_in, counts, lsem.at[8]),
    ]
    for cp in local[:2]:
        cp.start()
    barrier = pltpu.get_barrier_semaphore()
    peers = (sib, xm, pm, pmo, zp, zn)
    for t in peers:
        pl.semaphore_signal(barrier, inc=1, device_id=t, device_id_type=MESH)
    for cp in local[2:]:
        cp.start()

    local[0].wait()
    local[1].wait()
    row = lax.broadcasted_iota(jnp.int32, (KEPT, TRACKS * FRAMES), 0)
    src = lax.broadcasted_iota(jnp.int32, (KEPT, TRACKS * FRAMES), 1)
    notes = []
    for cam in range(CAMS):
        f0, f1 = fill[cam, 0], fill[cam, 1]
        full = jnp.where(f0 == FRAMES, 0, jnp.where(f1 == FRAMES, 1, 2))
        first = jnp.where(full == 0, 1, 0)
        second = jnp.where(full == 2, 1, 2)
        cut = jnp.where(full == 0, f1, f0)
        notes += [cut, full]
        want = jnp.where(
            row < HALF,
            full * FRAMES + row,
            jnp.where(row - HALF < cut, first * FRAMES + row - HALF, second * FRAMES + row - HALF - cut),
        )
        pick = (src == want).astype(jnp.float32).astype(jnp.bfloat16)
        kept = jnp.dot(pick, gv[cam].reshape(TRACKS * FRAMES, EMB), preferred_element_type=jnp.float32)
        gal[z, xi, cam] = kept.astype(jnp.bfloat16)
    line = lax.broadcasted_iota(jnp.int32, (8, 128), 0)
    meta[z, xi] = jnp.where(
        line == 0, notes[0], jnp.where(line == 1, notes[2], jnp.where(line == 2, notes[1], notes[3]))
    )
    pl.semaphore_wait(barrier, len(peers))

    sent = []

    def send(ref_from, ref_to, s_sem, r_sem, to):
        cp = pltpu.make_async_remote_copy(
            src_ref=ref_from, dst_ref=ref_to, send_sem=s_sem, recv_sem=r_sem, device_id=to, device_id_type=MESH
        )
        cp.start()
        sent.append(cp)

    def drain(keep):
        while len(sent) > keep:
            sent.pop(0).wait_send()

    def arrive(ref, s_sem, r_sem):
        pltpu.make_async_remote_copy(
            src_ref=ref, dst_ref=ref, send_sem=s_sem, recv_sem=r_sem, device_id=sib, device_id_type=MESH
        ).wait_recv()

    def unit(stream, zz, part):
        ref = gal.at[zz, 1 - xi if stream == 1 else xi, 1 if stream == 2 else 0]
        return ref if part is None else ref.at[pl.ds(part * HALF, HALF)]

    def note(stream, zz):
        return meta.at[zz]

    def noted(stream, way, hop):
        return stream == 1 and not (way == 1 and hop == 4)

    def z_send(stream, way, hop):
        ref = unit(stream, at(-(hop - 1) if way == 0 else hop - 1), way if hop == 4 else None)
        to = zp if way == 0 else zn
        send(ref, ref, zs.at[way, stream, hop - 1], zr.at[way, stream, hop - 1], to)
        if noted(stream, way, hop):
            ref = note(stream, at(-(hop - 1) if way == 0 else hop - 1))
            send(ref, ref, ms.at[way, hop - 1], mr.at[way, hop - 1], to)

    def x_unit(column, cam, hop, way):
        ref = gal.at[at(-hop if way == 0 else hop), column, cam]
        return ref.at[pl.ds(way * HALF, HALF)] if hop == 4 else ref

    def x_index(cam, hop, way):
        return 0 if cam == 0 else 1 if hop == 0 else 2 + (hop - 1) * 2 + way

    def x_send(cam, hop, way):
        k, ref = x_index(cam, hop, way), x_unit(xi, cam, hop, way)
        send(ref, ref, xs.at[k], xr.at[k], xm)
        if cam == 0:
            send(meta.at[z, xi], meta.at[z, xi], xs.at[10], xr.at[10], xm)

    def x_arrive(cam, hop, way):
        k = x_index(cam, hop, way)
        arrive(x_unit(1 - xi, cam, hop, way), xs.at[k], xr.at[k])
        if cam == 0:
            arrive(meta.at[z, 1 - xi], xs.at[10], xr.at[10])

    def z_arrive(stream, hop):
        for way in range(2):
            zz = at(-hop if way == 0 else hop)
            arrive(unit(stream, zz, way if hop == 4 else None), zs.at[way, stream, hop - 1], zr.at[way, stream, hop - 1])
            if noted(stream, way, hop):
                arrive(note(stream, zz), ms.at[way, hop - 1], mr.at[way, hop - 1])
            if hop < 4:
                z_send(stream, way, hop + 1)
            if stream == 2:
                x_send(1, hop, way)

    def embed(cam):
        rows = fv[cam].astype(jnp.float32) * sc[...].reshape(1, FEAT) + sh[...].reshape(1, FEAT)
        normed[...] = rows.astype(jnp.bfloat16)
        projected = jnp.dot(normed[...], pv[...], preferred_element_type=jnp.float32)
        total = jnp.sum(projected * projected, axis=-1, keepdims=True)
        unit_rows = (projected * lax.rsqrt(total + 1e-06)).astype(jnp.bfloat16)
        emb[0, cam] = unit_rows.T

    def emb_send(grp, cam):
        k, to = {2: (0, pm), 1: (1, sib)}[grp]
        send(emb.at[0, cam], emb.at[grp, cam], es.at[k, cam], er.at[k, cam], to)

    def emb_arrive(grp, cam):
        k = {2: 0, 1: 1, 3: 2}[grp]
        arrive(emb.at[grp, cam], es.at[k, cam], er.at[k, cam])
        if grp == 2:
            send(emb.at[2, cam], emb.at[3, cam], es.at[2, cam], er.at[2, cam], sib)

    def score(zz, grp, cam):
        sims = jnp.dot(
            gal[zz].reshape(4 * KEPT, EMB), emb[grp, cam], preferred_element_type=jnp.float32
        )
        frame = lax.broadcasted_iota(jnp.int32, (HALF, CROPS), 0)
        rows = []
        for q in range(4):
            cut = meta[zz, q // 2, pl.ds(q % 2, 1), :]
            full = meta[zz, q // 2, pl.ds(2 + q % 2, 1), :]
            cut = jnp.concatenate([cut, cut], axis=1)
            full = jnp.concatenate([full, full], axis=1)
            whole = sims[q * KEPT : q * KEPT + HALF]
            mixed = sims[q * KEPT + HALF : (q + 1) * KEPT]
            mine = frame < cut
            a = jnp.max(whole, axis=0, keepdims=True)
            u = jnp.max(jnp.where(mine, mixed, -jnp.inf), axis=0, keepdims=True)
            v = jnp.max(jnp.where(mine, -jnp.inf, mixed), axis=0, keepdims=True)
            rows.append(jnp.where(full == 0, a, u))
            rows.append(jnp.where(full == 1, a, jnp.where(full == 0, u, v)))
            rows.append(jnp.where(full == 2, a, v))
        rows.append(jnp.zeros((4, CROPS), jnp.float32))
        return jnp.concatenate(rows, axis=0)

    def work(places, grps, cams):
        ng, nc = grps[1] - grps[0], cams[1] - cams[0]

        def body(t, carry):
            i = places[0] + t // (ng * nc)
            grp, cam = grps[0] + (t // nc) % ng, cams[0] + t % nc
            d = jnp.where(i % 2 == 1, (i + 1) // 2, 0 - i // 2)
            res[grp, i, cam] = score(at(d), grp, cam)
            return carry

        count = (places[1] - places[0]) * ng * nc
        lax.fori_loop(0, count, body, 0, unroll=min(count, 4))

    def give_sib(k):
        lo, n = SIB_PARTS[k]
        send(res.at[1, pl.ds(lo, n)], rsr.at[pl.ds(lo, n)], ss.at[k], sr.at[k], sib)

    def give_pair(m):
        for t, to in enumerate((pm, pmo)):
            rows = [res[2 + t, i, cam][0:ROWS] for i, cam in MESSAGES[m]]
            rps[t, m] = jnp.concatenate(rows, axis=0).astype(jnp.bfloat16)
            send(rps.at[t, m], rpr.at[t, m], ps.at[t, m], pr.at[t, m], to)

    x_send(0, 0, 0)
    z_send(2, 0, 1)
    z_send(2, 1, 1)
    local[2].wait()
    local[3].wait()
    local[4].wait()
    local[5].wait()
    embed(0)
    emb_send(2, 0)
    z_send(0, 0, 1)
    z_send(0, 1, 1)
    x_send(1, 0, 0)
    emb_send(1, 0)
    local[6].wait()
    embed(1)
    emb_send(1, 1)
    x_arrive(0, 0, 0)
    z_send(1, 0, 1)
    z_send(1, 1, 1)

    local[7].wait()
    local[8].wait()
    n_row = lax.broadcasted_iota(jnp.int32, (NEIGH * TRACKS, NEIGH), 0)
    n_col = lax.broadcasted_iota(jnp.int32, (NEIGH * TRACKS, NEIGH), 1) * TRACKS
    same = (n_row >= n_col) & (n_row < n_col + TRACKS)
    for cam in range(CAMS):
        spread = jnp.where(same, av[pl.ds(cam, 1), :].astype(jnp.float32), 0.0).astype(jnp.bfloat16)
        adjc[cam] = jnp.dot(spread, jnp.ones((NEIGH, 128), jnp.bfloat16), preferred_element_type=jnp.float32)

    own, other, all_cams, pair = (0, 1), (1, 2), (0, 2), (2, 4)
    z_arrive(2, 1)
    emb_send(2, 1)
    z_arrive(0, 1)
    x_arrive(1, 0, 0)
    emb_arrive(1, 0)
    emb_arrive(1, 1)
    work((0, 1), (0, 2), all_cams)
    z_arrive(1, 1)
    z_arrive(2, 2)
    x_arrive(1, 1, 0)
    x_arrive(1, 1, 1)
    work((1, 3), own, all_cams)
    z_arrive(0, 2)
    work((1, 3), other, all_cams)
    emb_arrive(2, 0)
    z_arrive(1, 2)
    z_arrive(2, 3)
    emb_arrive(3, 0)
    work((0, 3), pair, (0, 1))
    x_arrive(1, 2, 0)
    x_arrive(1, 2, 1)
    work((3, 4), pair, (0, 1))
    give_pair(0)
    z_arrive(0, 3)
    work((3, 5), own, all_cams)
    work((4, 5), pair, (0, 1))
    emb_arrive(2, 1)
    z_arrive(1, 3)
    work((3, 5), other, all_cams)
    give_sib(0)
    z_arrive(2, 4)
    emb_arrive(3, 1)
    work((0, 4), pair, (1, 2))
    give_pair(1)
    x_arrive(1, 3, 0)
    x_arrive(1, 3, 1)
    work((4, 5), pair, (1, 2))
    work((5, 6), pair, all_cams)
    give_pair(2)
    z_arrive(0, 4)
    work((6, 7), pair, all_cams)
    work((5, 7), (0, 2), all_cams)
    give_sib(1)
    drain(20)
    z_arrive(1, 4)
    x_arrive(1, 4, 0)
    x_arrive(1, 4, 1)
    work((7, 8), pair, all_cams)
    give_pair(3)
    work((7, 8), other, all_cams)
    give_sib(2)
    work((7, 8), own, all_cams)
    drain(6)

    def weave(even, odd):
        return jnp.concatenate([even[0:6], odd[0:6], even[6:12], odd[6:12]], axis=0)

    lane = lax.broadcasted_iota(jnp.int32, (24, CROPS), 1)

    def finish(i, sides=(0, 1)):
        zz = at(DELTA[i])
        for cam in range(CAMS):
            m, j = PLACE[i, cam]
            for side in sides:
                if side == 0:
                    here, there = res[0, i, cam], rsr[i, cam]
                else:
                    here, there = [rpr[t, m, j * ROWS : (j + 1) * ROWS].astype(jnp.float32) for t in range(2)]
                block = weave(jnp.where(c == 0, here, there), jnp.where(c == 0, there, here))
                cls = x // 2 if side == 0 else 1 - x // 2
                at_row = pl.multiple_of(zz * 48 + cls * 24, 8)
                factor = adjc[cam, pl.ds(at_row, 24), :]
                block = block * jnp.concatenate([factor, factor], axis=1)
                out[cam, pl.ds(at_row, 24), :] = jnp.where(lane < counts[cam], block, 0.0)

    def pair_arrive(m):
        for t in range(2):
            arrive(rpr.at[t, m], ps.at[t, m], pr.at[t, m])

    def sib_arrive(k):
        lo, n = SIB_PARTS[k]
        arrive(rsr.at[pl.ds(lo, n)], ss.at[k], sr.at[k])

    sib_arrive(0)
    pair_arrive(0)
    pair_arrive(1)
    for i in range(4):
        finish(i)
    sib_arrive(1)
    pair_arrive(2)
    for i in (4, 5):
        finish(i)
    sib_arrive(2)
    for i in (6, 7):
        finish(i, (0,))
    drain(2)
    pair_arrive(3)
    for i in (6, 7):
        finish(i, (1,))
    drain(0)


def per_device(feat, counts, scale, shift, proj, gall, fill, adj):
    hbm = pl.BlockSpec(memory_space=pltpu.HBM)
    bf, f32, dma = jnp.bfloat16, jnp.float32, pltpu.SemaphoreType.DMA
    return pl.pallas_call(
        kernel,
        name="match",
        out_shape=pltpu.VMEM((CAMS, NEIGH * TRACKS, CROPS), f32),
        in_specs=[hbm] * 8,
        out_specs=pl.BlockSpec(memory_space=pltpu.VMEM),
        scratch_shapes=[
            pltpu.SMEM((CAMS,), jnp.int32),
            pltpu.SMEM((CAMS, TRACKS), jnp.int32),
            pltpu.VMEM((CAMS, CROPS, FEAT), bf),
            pltpu.VMEM((FEAT, EMB), bf),
            pltpu.VMEM((CAMS, TRACKS, FRAMES, EMB), bf),
            pltpu.VMEM((FEAT,), f32),
            pltpu.VMEM((FEAT,), f32),
            pltpu.VMEM((CAMS, NEIGH), jnp.int32),
            pltpu.VMEM((CAMS, NEIGH * TRACKS, 128), f32),
            pltpu.VMEM((CROPS, FEAT), bf),
            pltpu.VMEM((NZ, 2, CAMS, KEPT, EMB), bf),
            pltpu.VMEM((NZ, 2, 8, 128), jnp.int32),
            pltpu.VMEM((4, CAMS, EMB, CROPS), bf),
            pltpu.VMEM((4, NZ, CAMS, 16, CROPS), f32),
            pltpu.VMEM((NZ, CAMS, 16, CROPS), f32),
            pltpu.VMEM((2, 4, 4 * ROWS, CROPS), bf),
            pltpu.VMEM((2, 4, 4 * ROWS, CROPS), bf),
            dma((9,)),
            dma((2, 3, 4)),
            dma((2, 3, 4)),
            dma((2, 4)),
            dma((2, 4)),
            dma((11,)),
            dma((11,)),
            dma((3, CAMS)),
            dma((3, CAMS)),
            dma((3,)),
            dma((3,)),
            dma((2, 4)),
            dma((2, 4)),
        ],
        compiler_params=pltpu.CompilerParams(
            collective_id=0, has_side_effects=True, vmem_limit_bytes=60 * 2**20
        ),
    )(feat, counts, scale, shift, proj, gall, fill, adj)


def solution(mesh):
    return jax.shard_map(
        per_device,
        mesh=mesh,
        in_specs=(
            P(("region", "stream"), None, None),
            P(("region", "stream")),
            P(),
            P(),
            P(),
            P(("region", "stream"), None, None, None),
            P(("region", "stream"), None),
            P(("region", "stream"), None),
        ),
        out_specs=P(("region", "stream"), None, None),
        check_vma=False,
    )
```
